32 devices in a mesh: row: 2 (over x), col: 4 (over z), layer: 4 (over y, core).
Axes of the slice: x: 2, y: 2, z: 4, core: 2. Of those that a mesh axis runs over, the one named last changes fastest.
Arguments:
- a_blocks: bfloat16 [64, 128, 128], P(('row', 'col', 'layer')), may hold values from -0.5 to 0.5
- a_slot: int32 [64], P(('row', 'col', 'layer')), may hold values from 0 to 63, as said below
- b_blocks: bfloat16 [32, 128, 128], P(('row', 'col', 'layer')), may hold values from -6 to 6
- b_slot: int32 [32], P(('row', 'col', 'layer')), may hold values from 0 to 31, as said below
- c_mask: int32 [32, 32], P('row', 'col'), may hold values from 0 to 1, as said below
Outputs:
- product: float32 [4096, 4096], P(('row', 'layer'), 'col')
The draws below stay inside these ranges and needn't reach their ends.
Inputs may be any that keep to these rules, and one draw needn't show every extreme that they name: `a_slot`: within each row panel r and inner slice l the 8 slots of A are distinct. `b_slot`: within each column panel c and inner slice l the 2 slots of B are distinct. `c_mask`: every block row has exactly 4 ones in each column panel of 8 block columns.
All inputs are finite; a program needn't handle non-finite values.
Results may differ from the reference program's by a relative error of at most 0.0003.
Values may be sent and summed in bfloat16 or wider, within the bound.
No kernel may reach another device: no remote copies, remote signals or barrier semaphores. Data moves between devices by JAX's collectives and lax.ppermute only.
A program may use at most 64 MiB of HBM per device.

```python
import jax
import jax.numpy as jnp

BS = 128
MBP = 16
KBL = 4
NBP = 8
NA_DEV = 2
NB_DEV = 1
MB = 32
KB = 16
NB = 32
NAE = 64
NBE = 32
N_ROW = 2
N_COL = 4
N_LAYER = 4


def draw_a_slot(key, part):
    key = jax.random.fold_in(key, 11)
    keys = jax.random.split(key, N_ROW * N_LAYER)
    perms = jax.vmap(lambda k: jax.random.permutation(k, MBP * KBL))(keys)
    taken = perms[:, :N_COL * NA_DEV].reshape(N_ROW, N_LAYER, N_COL, NA_DEV)
    return taken.transpose(0, 2, 1, 3).reshape(-1).astype(jnp.int32)


def draw_b_slot(key, part):
    key = jax.random.fold_in(key, 23)
    keys = jax.random.split(key, N_COL * N_LAYER)
    perms = jax.vmap(lambda k: jax.random.permutation(k, KBL * NBP))(keys)
    taken = perms[:, :N_ROW * NB_DEV].reshape(N_COL, N_LAYER, N_ROW, NB_DEV)
    return taken.transpose(2, 0, 1, 3).reshape(-1).astype(jnp.int32)


def draw_c_mask(key, part):
    key = jax.random.fold_in(key, 37)
    keys = jax.random.split(key, MB * N_COL)
    perms = jax.vmap(lambda k: jax.random.permutation(k, NBP))(keys)
    return (perms < NBP // 2).astype(jnp.int32).reshape(MB, NB)


def levels(rng, shape, cuts, low, top_value):
    def one(position, parts):
        steps = jax.random.uniform(jax.random.fold_in(jax.random.fold_in(rng, 6), position), (parts,), jnp.float32, low / len(cuts), top_value / len(cuts))
        return jnp.repeat(jnp.exp(steps), shape[position] // parts).reshape((-1,) + (1,) * (len(shape) - position - 1))

    factor_of = one(*cuts[0])
    for cut in cuts[1:]:
        factor_of = factor_of * one(*cut)
    return factor_of


def scatter_about(stream_key, dims, width, limit, pieces=(), held_as=jnp.bfloat16):
    entries = jax.random.normal(stream_key, dims, jnp.float32) * width
    if len(pieces) > 0:
        entries = levels(stream_key, dims, pieces, -0.22, 0.18) * entries
    return jnp.clip(entries, min=-limit, max=limit).astype(held_as)


def setup_inputs(seed: int = 0) -> dict:
    splits = jax.random.split(jax.random.key(seed), 6)
    return {
        "a_blocks": scatter_about(splits[0], (NAE, BS, BS), (BS * KB // 16) ** -0.5, 0.5, ((0, 32),)),
        "a_slot": draw_a_slot(jax.random.fold_in(splits[5], 71), 0),
        "b_blocks": scatter_about(splits[2], (NBE, BS, BS), 1.0, 6.0, ((0, 32),)),
        "b_slot": draw_b_slot(jax.random.fold_in(splits[5], 71), 0),
        "c_mask": draw_c_mask(jax.random.fold_in(splits[5], 71), 0),
    }


def reference(a_blocks, a_slot, b_blocks, b_slot, c_mask):
    a_index = (jnp.arange(NAE) // NA_DEV).astype(jnp.int32)
    a_layer = a_index % N_LAYER
    a_row = (a_index // N_LAYER) // N_COL
    row_block = a_row * MBP + a_slot // KBL
    inner_a = a_layer * KBL + a_slot % KBL
    dense_a = jnp.zeros((MB, KB, BS, BS), jnp.bfloat16).at[row_block, inner_a].set(a_blocks)
    a_matrix = dense_a.transpose(0, 2, 1, 3).reshape(MB * BS, KB * BS)
    b_index = (jnp.arange(NBE) // NB_DEV).astype(jnp.int32)
    b_layer = b_index % N_LAYER
    b_col = (b_index // N_LAYER) % N_COL
    inner_b = b_layer * KBL + b_slot // NBP
    col_block = b_col * NBP + b_slot % NBP
    dense_b = jnp.zeros((KB, NB, BS, BS), jnp.bfloat16).at[inner_b, col_block].set(b_blocks)
    b_matrix = dense_b.transpose(0, 2, 1, 3).reshape(KB * BS, NB * BS)
    full = jnp.dot(a_matrix, b_matrix, preferred_element_type=jnp.float32)
    keep = jnp.broadcast_to(c_mask.astype(jnp.float32)[:, None, :, None], (MB, BS, NB, BS))
    return full * keep.reshape(MB * BS, NB * BS)
```

```python
import functools

import jax
import jax.numpy as jnp
from jax import lax
from jax.experimental import pallas as pl
from jax.experimental.pallas import tpu as pltpu
from jax.sharding import PartitionSpec as P

MBP = 16
KBL = 4
NBP = 8
CORES = 2
A_BITS = 17
B_BITS = 5
TILE = 16
ANYWHERE = pl.BlockSpec(memory_space=pl.ANY)
IN_VMEM = pl.BlockSpec(memory_space=pltpu.VMEM)


def blank_kernel(out_ref, blank, sems):
    rows = blank.shape[0]
    blank[...] = jnp.zeros_like(blank)
    copies = []
    for i in range(out_ref.shape[0] // rows):
        copies.append(pltpu.make_async_copy(blank, out_ref.at[i * rows : (i + 1) * rows], sems.at[i]))
        copies[-1].start()
    for copy in copies:
        copy.wait()


def blank_output(rows, width):
    shape = (rows * width, NBP * width)
    return pl.pallas_call(
        blank_kernel,
        out_shape=jax.ShapeDtypeStruct(shape, jnp.float32),
        out_specs=ANYWHERE,
        scratch_shapes=[pltpu.VMEM((width, NBP * width), jnp.float32), pltpu.SemaphoreType.DMA((rows,))],
        cost_estimate=pl.CostEstimate(flops=0, bytes_accessed=2097152, transcendentals=0),
        compiler_params=pltpu.CompilerParams(vmem_limit_bytes=16 * 2**20),
    )()


def multiply_kernel(
    sizes, mask_hbm, blocks, blank_ref, out_ref, mask, slot_rows, slots, row_bits, pairs, acc, sems, out_sems
):
    del blank_ref
    n_layer, n_col, n_row, n_a, n_b = sizes
    width = blocks.shape[-1]
    own_rows = MBP // n_layer
    first_row = lax.axis_index("layer") * own_rows
    a_part = n_a * width + TILE
    b_part = n_b * width + TILE
    a_starts = [0] + [b_part + i * a_part for i in range(1, n_col)]
    b_starts = [a_part] + [n_col * a_part + i * b_part for i in range(1, n_row)]
    stride = n_col * a_part + n_row * b_part
    tile_starts = [at + n_a * width for at in a_starts] + [at + n_b * width for at in b_starts]
    tiles = len(tile_starts)

    mask_copy = pltpu.make_async_copy(mask_hbm, mask, sems.at[0])
    mask_copy.start()
    for q in range(n_layer):
        for i, start in enumerate(tile_starts):
            at = q * stride + start
            tile = blocks[at : at + TILE, :].astype(jnp.float32)
            slot_rows[q * tiles + i, :] = tile[0].astype(jnp.int32)
    slot_copy = pltpu.make_async_copy(slot_rows, slots, sems.at[1])
    slot_copy.start()
    mask_copy.wait()
    for row in range(own_rows):
        bits = mask[0, first_row + row]
        for col in range(1, NBP):
            bits = bits | lax.shift_left(mask[col, first_row + row], col)
        row_bits[row] = bits
    slot_copy.wait()

    def scan(q, count):
        base = q * tiles
        words = []
        for i, start in enumerate(a_starts):
            for t in range(n_a):
                s = slots[base + i, t]
                row = lax.shift_right_logical(s, KBL.bit_length() - 1) - first_row
                near = jnp.clip(row, 0, own_rows - 1)
                bits = jnp.where(row == near, row_bits[near], 0)
                word = lax.shift_left(bits, (s & (KBL - 1)) * NBP)
                at = q * (stride // TILE) + (start + t * width) // TILE
                words.append((word, lax.shift_left(at, A_BITS) + near * NBP))
        for i, start in enumerate(b_starts):
            for t in range(n_b):
                s = slots[base + n_col + i, t]
                at = q * (stride // TILE) + (start + t * width) // TILE
                b_code = lax.shift_left(at, B_BITS) + (s & (NBP - 1))
                for word, a_code in words:
                    pairs[count] = a_code + b_code
                    count = count + (lax.shift_right_logical(word, s) & 1)
        return count

    count = lax.fori_loop(0, n_layer, scan, jnp.int32(0), unroll=n_layer <= 4)
    pairs[count] = 0

    def copy_of(here):
        row = lax.shift_right_logical(here, NBP.bit_length() - 1)
        col = here & (NBP - 1)
        return pltpu.make_async_copy(
            acc.at[here],
            out_ref.at[
                pl.ds(pl.multiple_of(row * width, width), width),
                pl.ds(pl.multiple_of(col * width, width), width),
            ],
            out_sems.at[here],
        )

    def block(at):
        return blocks[pl.ds(pl.multiple_of(at * TILE, TILE), width), :]

    def product(code):
        a_at = lax.shift_right_logical(code, A_BITS)
        b_at = lax.shift_right_logical(code, B_BITS) & (2 ** (A_BITS - B_BITS) - 1)
        return jnp.dot(block(a_at), block(b_at), preferred_element_type=jnp.float32)

    def put(code, value, seen):
        here = code & (2**B_BITS - 1)
        bit = lax.shift_left(jnp.int32(1), here)
        first = (seen & bit) == 0

        @pl.when(first)
        def _():
            acc[here] = value

        @pl.when(jnp.logical_not(first))
        def _():
            copy_of(here).wait()
            acc[here] += value

        copy_of(here).start()
        return seen | bit

    def two_products(n, seen):
        codes = [pairs[2 * n], pairs[2 * n + 1]]
        values = [product(code) for code in codes]
        seen = put(codes[0], values[0], seen)
        return lax.cond(2 * n + 1 < count, lambda: put(codes[1], values[1], seen), lambda: seen)

    seen = lax.fori_loop(0, lax.shift_right_logical(count + 1, 1), two_products, jnp.int32(0))

    def settle(n, left):
        here = pairs[n] & (2**B_BITS - 1)
        bit = lax.shift_left(jnp.int32(1), here)

        @pl.when((left & bit) != 0)
        def _():
            copy_of(here).wait()

        return left & ~bit

    lax.fori_loop(0, count, settle, seen)


def multiply(blocks, mask_t, blank, n_a, n_b):
    n_layer, n_col, n_row = (lax.axis_size(name) for name in ("layer", "col", "row"))
    own_rows = MBP // n_layer
    width = blocks.shape[-1]
    n_pairs = n_layer * n_col * n_a * n_row * n_b
    slot_shape = (n_layer * (n_col + n_row), width)
    return pl.pallas_call(
        functools.partial(multiply_kernel, (n_layer, n_col, n_row, n_a, n_b)),
        out_shape=jax.ShapeDtypeStruct(blank.shape, blank.dtype),
        in_specs=[ANYWHERE, IN_VMEM, ANYWHERE],
        out_specs=ANYWHERE,
        scratch_shapes=[
            pltpu.SMEM(mask_t.shape, jnp.int32),
            pltpu.VMEM(slot_shape, jnp.int32),
            pltpu.SMEM(slot_shape, jnp.int32),
            pltpu.SMEM((own_rows,), jnp.int32),
            pltpu.SMEM((n_pairs + 2,), jnp.int32),
            pltpu.VMEM((own_rows * NBP, width, width), jnp.float32),
            pltpu.SemaphoreType.DMA((2,)),
            pltpu.SemaphoreType.DMA((own_rows * NBP,)),
        ],
        input_output_aliases={2: 0},
        compiler_params=pltpu.CompilerParams(vmem_limit_bytes=48 * 2**20),
    )(mask_t, blocks, blank)


def shift(value, axis, step):
    size = lax.axis_size(axis)
    return lax.ppermute(value, axis, [(i, (i + step) % size) for i in range(size)])


def to_other_core(value):
    size = lax.axis_size("layer")
    return lax.ppermute(value, "layer", [(i, i ^ 1) for i in range(size)])


def pack_kernel(a_hbm, slot_hbm, b_hbm, out, slots, sems):
    a_rows = a_hbm.shape[0]
    moves = ((slot_hbm, slots), (a_hbm, out.at[:a_rows]), (b_hbm, out.at[a_rows + TILE :]))
    copies = [pltpu.make_async_copy(x, y, sems.at[i]) for i, (x, y) in enumerate(moves)]
    for copy in copies:
        copy.start()
    lane = lax.broadcasted_iota(jnp.int32, (TILE, out.shape[-1]), 1)
    copies[0].wait()
    tile = jnp.zeros(lane.shape, jnp.int32)
    for i in range(slots.shape[0]):
        tile = jnp.where(lane == i, slots[i], tile)
    out[a_rows : a_rows + TILE, :] = tile.astype(jnp.float32).astype(out.dtype)
    copies[1].wait()
    copies[2].wait()


def pack(a_blocks, a_slot, b_blocks):
    width = a_blocks.shape[-1]
    args = [a_blocks.reshape(-1, width), a_slot, b_blocks.reshape(-1, width)]
    a, a_slot, b = [pltpu.with_memory_space_constraint(x, pltpu.HBM) for x in args]
    return pl.pallas_call(
        pack_kernel,
        out_shape=jax.ShapeDtypeStruct((a.shape[0] + TILE + b.shape[0], width), a.dtype),
        in_specs=[pl.BlockSpec(memory_space=pltpu.HBM)] * 3,
        out_specs=IN_VMEM,
        scratch_shapes=[pltpu.SMEM(a_slot.shape, jnp.int32), pltpu.SemaphoreType.DMA((3,))],
        compiler_params=pltpu.CompilerParams(vmem_limit_bytes=16 * 2**20),
    )(a, a_slot, b)


def slot_tile(slots, width, dtype):
    row = slots.astype(dtype)[None, :]
    return jnp.pad(row, ((0, TILE - 1), (0, width - slots.shape[0])))


def joined(parts):
    return jnp.concatenate(parts, axis=0) if len(parts) > 1 else parts[0]


def split(value, likes):
    parts, at = [], 0
    for like in likes:
        parts.append(lax.slice_in_dim(value, at, at + like.shape[0], axis=0))
        at += like.shape[0]
    return parts


def on_device(a_blocks, a_slot, b_blocks, b_slot, c_mask):
    n_layer, n_col, n_row = (lax.axis_size(name) for name in ("layer", "col", "row"))
    n_a, n_b = a_blocks.shape[0], b_blocks.shape[0]
    far = range(CORES, n_layer, CORES)
    middle = n_col // 2
    sides = [s for s in range(1, n_col) if s != middle]

    width = a_blocks.shape[-1]
    a_rows = n_a * width + TILE
    packed = pack(a_blocks, a_slot, b_blocks)
    a_own = packed[:a_rows]
    own = joined([packed, slot_tile(b_slot, width, a_own.dtype)])

    a_sides = [shift(a_own, "col", s) for s in sides]
    a_middle = shift(a_own, "col", middle)
    blank = blank_output(MBP // n_layer, width)
    a_sides, blank = lax.optimization_barrier((a_sides, blank))
    own_far = [shift(own, "layer", s) for s in far]
    side_pair = joined(a_sides)
    sides_far = [shift(side_pair, "layer", s) for s in far]
    late = joined([a_middle, own_far[0][-TILE:]])
    middle_far = [shift(late, "layer", s)[:a_rows] for s in far]
    b_line = joined([p[a_rows:] for p in [own] + own_far])
    b_across = [shift(b_line, "row", s) for s in range(1, n_row)]

    b_rows = own.shape[0] - a_rows
    near = {(j, 0, 0): p for j, p in enumerate([own] + own_far)}
    near |= {(0, 1, 0): side_pair, (0, 1, 1): a_middle}
    for i, p in enumerate(b_across):
        near |= {(j, 2, i): p[j * b_rows : (j + 1) * b_rows] for j in range(1 + len(far))}
    distant = {}
    for j in range(len(far)):
        distant |= {(1 + j, 1, 0): sides_far[j], (1 + j, 1, 1): middle_far[j]}
    pools = [near, distant]
    here = [lax.optimization_barrier(joined(list(pool.values()))) for pool in pools]
    other = [to_other_core(p) for p in here]

    def in_order(wholes):
        parts = {}
        for pool, whole in zip(pools, wholes):
            parts |= dict(zip(pool, split(whole, pool.values())))
        return [parts[key] for key in sorted(parts)]

    blocks = joined(in_order(here) + in_order(other))
    return multiply(blocks, c_mask.T, blank, n_a, n_b)


def solution(mesh):
    in_specs = (
        P(("row", "col", "layer"), None, None),
        P(("row", "col", "layer")),
        P(("row", "col", "layer"), None, None),
        P(("row", "col", "layer")),
        P("row", "col"),
    )
    out_specs = P(("row", "layer"), "col")
    return jax.shard_map(
        on_device, mesh=mesh, in_specs=in_specs, out_specs=out_specs, check_vma=False
    )
```

```python
import functools

import jax
import jax.numpy as jnp
from jax import lax
from jax.experimental import pallas as pl
from jax.experimental.pallas import tpu as pltpu
from jax.sharding import PartitionSpec as P

MBP = 16
KBL = 4
NBP = 8
CORES = 2
A_BITS = 17
B_BITS = 5
TILE = 16
LANES = 8
ANYWHERE = pl.BlockSpec(memory_space=pl.ANY)
IN_VMEM = pl.BlockSpec(memory_space=pltpu.VMEM)


def blank_kernel(out_ref, blank, sems):
    rows = blank.shape[0]
    blank[...] = jnp.zeros_like(blank)
    copies = []
    for i in range(out_ref.shape[0] // rows):
        copies.append(pltpu.make_async_copy(blank, out_ref.at[i * rows : (i + 1) * rows], sems.at[i]))
        copies[-1].start()
    for copy in copies:
        copy.wait()


def blank_output(rows, width):
    shape = (rows * width, NBP * width)
    return pl.pallas_call(
        blank_kernel,
        out_shape=jax.ShapeDtypeStruct(shape, jnp.float32),
        out_specs=ANYWHERE,
        scratch_shapes=[pltpu.VMEM((width, NBP * width), jnp.float32), pltpu.SemaphoreType.DMA((rows,))],
        cost_estimate=pl.CostEstimate(flops=0, bytes_accessed=2097152, transcendentals=0),
        compiler_params=pltpu.CompilerParams(vmem_limit_bytes=16 * 2**20),
    )()


def multiply_kernel(
    sizes, mask_hbm, blocks, blank_ref, out_ref, mask, slot_rows, slots, row_bits, pairs, acc, sems, out_sems
):
    del blank_ref
    n_layer, n_col, n_row, n_a, n_b = sizes
    width = blocks.shape[-1]
    own_rows = MBP // n_layer
    first_row = lax.axis_index("layer") * own_rows
    a_part = n_a * width + TILE
    b_part = n_b * width + TILE
    a_starts = [0] + [b_part + i * a_part for i in range(1, n_col)]
    b_starts = [a_part] + [n_col * a_part + i * b_part for i in range(1, n_row)]
    stride = n_col * a_part + n_row * b_part
    tile_starts = [at + n_a * width for at in a_starts] + [at + n_b * width for at in b_starts]

    mask_copy = pltpu.make_async_copy(mask_hbm, mask, sems.at[0])
    mask_copy.start()
    for q in range(n_layer):
        row = jnp.zeros((TILE // 2, width), jnp.float32)
        for i, start in enumerate(tile_starts):
            at = q * stride + start
            tile = blocks[at : at + TILE, :].astype(jnp.float32)[: TILE // 2]
            row = row + (pltpu.roll(tile, i * LANES, 1) if i else tile)
        slot_rows[q, :] = row[0].astype(jnp.int32)
    slot_copy = pltpu.make_async_copy(slot_rows, slots, sems.at[1])
    slot_copy.start()
    mask_copy.wait()
    for row in range(own_rows):
        bits = mask[0, first_row + row]
        for col in range(1, NBP):
            bits = bits | lax.shift_left(mask[col, first_row + row], col)
        row_bits[row] = bits
    slot_copy.wait()

    def scan(q, count):
        words = []
        for i, start in enumerate(a_starts):
            for t in range(n_a):
                s = slots[q, i * LANES + t]
                row = lax.shift_right_logical(s, KBL.bit_length() - 1) - first_row
                near = jnp.clip(row, 0, own_rows - 1)
                bits = jnp.where(row == near, row_bits[near], 0)
                word = lax.shift_left(bits, (s & (KBL - 1)) * NBP)
                at = q * (stride // TILE) + (start + t * width) // TILE
                words.append((word, lax.shift_left(at, A_BITS) + near * NBP))
        for i, start in enumerate(b_starts):
            for t in range(n_b):
                s = slots[q, (n_col + i) * LANES + t]
                at = q * (stride // TILE) + (start + t * width) // TILE
                b_code = lax.shift_left(at, B_BITS) + (s & (NBP - 1))
                for word, a_code in words:
                    pairs[count] = a_code + b_code
                    count = count + (lax.shift_right_logical(word, s) & 1)
        return count

    count = lax.fori_loop(0, n_layer, scan, jnp.int32(0), unroll=n_layer <= 4)
    pairs[count] = 0

    def copy_of(here):
        row = lax.shift_right_logical(here, NBP.bit_length() - 1)
        col = here & (NBP - 1)
        return pltpu.make_async_copy(
            acc.at[here],
            out_ref.at[
                pl.ds(pl.multiple_of(row * width, width), width),
                pl.ds(pl.multiple_of(col * width, width), width),
            ],
            out_sems.at[here],
        )

    def block(at):
        return blocks[pl.ds(pl.multiple_of(at * TILE, TILE), width), :]

    def product(code):
        a_at = lax.shift_right_logical(code, A_BITS)
        b_at = lax.shift_right_logical(code, B_BITS) & (2 ** (A_BITS - B_BITS) - 1)
        return jnp.dot(block(a_at), block(b_at), preferred_element_type=jnp.float32)

    def put(code, value, seen):
        here = code & (2**B_BITS - 1)
        bit = lax.shift_left(jnp.int32(1), here)
        first = (seen & bit) == 0

        @pl.when(first)
        def _():
            acc[here] = value

        @pl.when(jnp.logical_not(first))
        def _():
            copy_of(here).wait()
            acc[here] += value

        copy_of(here).start()
        return seen | bit

    def two_products(n, seen):
        codes = [pairs[2 * n], pairs[2 * n + 1]]
        values = [product(code) for code in codes]
        seen = put(codes[0], values[0], seen)
        return lax.cond(2 * n + 1 < count, lambda: put(codes[1], values[1], seen), lambda: seen)

    seen = lax.fori_loop(0, lax.shift_right_logical(count + 1, 1), two_products, jnp.int32(0))

    def settle(n, left):
        here = pairs[n] & (2**B_BITS - 1)
        bit = lax.shift_left(jnp.int32(1), here)

        @pl.when((left & bit) != 0)
        def _():
            copy_of(here).wait()

        return left & ~bit

    lax.fori_loop(0, count, settle, seen)


def multiply(blocks, mask_t, blank, n_a, n_b):
    n_layer, n_col, n_row = (lax.axis_size(name) for name in ("layer", "col", "row"))
    own_rows = MBP // n_layer
    width = blocks.shape[-1]
    n_pairs = n_layer * n_col * n_a * n_row * n_b
    slot_shape = (n_layer, width)
    return pl.pallas_call(
        functools.partial(multiply_kernel, (n_layer, n_col, n_row, n_a, n_b)),
        out_shape=jax.ShapeDtypeStruct(blank.shape, blank.dtype),
        in_specs=[ANYWHERE, IN_VMEM, ANYWHERE],
        out_specs=ANYWHERE,
        scratch_shapes=[
            pltpu.SMEM(mask_t.shape, jnp.int32),
            pltpu.VMEM(slot_shape, jnp.int32),
            pltpu.SMEM(slot_shape, jnp.int32),
            pltpu.SMEM((own_rows,), jnp.int32),
            pltpu.SMEM((n_pairs + 2,), jnp.int32),
            pltpu.VMEM((own_rows * NBP, width, width), jnp.float32),
            pltpu.SemaphoreType.DMA((2,)),
            pltpu.SemaphoreType.DMA((own_rows * NBP,)),
        ],
        input_output_aliases={2: 0},
        compiler_params=pltpu.CompilerParams(vmem_limit_bytes=48 * 2**20),
    )(mask_t, blocks, blank)


def shift(value, axis, step):
    size = lax.axis_size(axis)
    return lax.ppermute(value, axis, [(i, (i + step) % size) for i in range(size)])


def to_other_core(value):
    size = lax.axis_size("layer")
    return lax.ppermute(value, "layer", [(i, i ^ 1) for i in range(size)])


def pack_kernel(a_hbm, slot_hbm, b_hbm, out, slots, sems):
    a_rows = a_hbm.shape[0]
    moves = ((slot_hbm, slots), (a_hbm, out.at[:a_rows]), (b_hbm, out.at[a_rows + TILE :]))
    copies = [pltpu.make_async_copy(x, y, sems.at[i]) for i, (x, y) in enumerate(moves)]
    for copy in copies:
        copy.start()
    lane = lax.broadcasted_iota(jnp.int32, (TILE, out.shape[-1]), 1)
    copies[0].wait()
    tile = jnp.zeros(lane.shape, jnp.int32)
    for i in range(slots.shape[0]):
        tile = jnp.where(lane == i, slots[i], tile)
    out[a_rows : a_rows + TILE, :] = tile.astype(jnp.float32).astype(out.dtype)
    copies[1].wait()
    copies[2].wait()


def pack(a_blocks, a_slot, b_blocks):
    width = a_blocks.shape[-1]
    args = [a_blocks.reshape(-1, width), a_slot, b_blocks.reshape(-1, width)]
    a, a_slot, b = [pltpu.with_memory_space_constraint(x, pltpu.HBM) for x in args]
    return pl.pallas_call(
        pack_kernel,
        out_shape=jax.ShapeDtypeStruct((a.shape[0] + TILE + b.shape[0], width), a.dtype),
        in_specs=[pl.BlockSpec(memory_space=pltpu.HBM)] * 3,
        out_specs=IN_VMEM,
        scratch_shapes=[pltpu.SMEM(a_slot.shape, jnp.int32), pltpu.SemaphoreType.DMA((3,))],
        compiler_params=pltpu.CompilerParams(vmem_limit_bytes=16 * 2**20),
    )(a, a_slot, b)


def slot_tile(slots, width, dtype):
    row = slots.astype(dtype)[None, :]
    return jnp.pad(row, ((0, TILE - 1), (0, width - slots.shape[0])))


def joined(parts):
    return jnp.concatenate(parts, axis=0) if len(parts) > 1 else parts[0]


def split(value, likes):
    parts, at = [], 0
    for like in likes:
        parts.append(lax.slice_in_dim(value, at, at + like.shape[0], axis=0))
        at += like.shape[0]
    return parts


def on_device(a_blocks, a_slot, b_blocks, b_slot, c_mask):
    n_layer, n_col, n_row = (lax.axis_size(name) for name in ("layer", "col", "row"))
    n_a, n_b = a_blocks.shape[0], b_blocks.shape[0]
    far = range(CORES, n_layer, CORES)
    width = a_blocks.shape[-1]
    a_rows = n_a * width + TILE
    packed = pack(a_blocks, a_slot, b_blocks)
    own = joined([packed, slot_tile(b_slot, width, packed.dtype)])
    own = lax.optimization_barrier(own)

    steps = sorted(range(1, n_col), key=lambda s: s != n_col // 2)
    a_sides = [shift(packed[:a_rows], "col", s) for s in steps[:-1]]
    a_last = shift(own[:a_rows], "col", steps[-1])
    blank = blank_output(MBP // n_layer, width)
    a_sides, blank = lax.optimization_barrier((a_sides, blank))
    own_far = [shift(own, "layer", s) for s in far]
    side_pair = joined(a_sides)
    sides_far = [shift(side_pair, "layer", s) for s in far]
    late = joined([a_last, own_far[0][-TILE:]])
    last_far = [shift(late, "layer", s)[:a_rows] for s in far]
    b_line = joined([p[a_rows:] for p in [own] + own_far])
    b_across = [shift(b_line, "row", s) for s in range(1, n_row)]

    b_rows = own.shape[0] - a_rows
    near = {(j, 0, 0): p for j, p in enumerate([own] + own_far)}
    near |= {(0, 1, 0): side_pair, (0, 1, 1): a_last}
    for i, p in enumerate(b_across):
        near |= {(j, 2, i): p[j * b_rows : (j + 1) * b_rows] for j in range(1 + len(far))}
    distant = {}
    for j in range(len(far)):
        distant |= {(1 + j, 1, 0): sides_far[j], (1 + j, 1, 1): last_far[j]}
    pools = [near, distant]
    here = [lax.optimization_barrier(joined(list(pool.values()))) for pool in pools]
    other = [to_other_core(p) for p in here]

    def in_order(wholes):
        parts = {}
        for pool, whole in zip(pools, wholes):
            parts |= dict(zip(pool, split(whole, pool.values())))
        return [parts[key] for key in sorted(parts)]

    blocks = joined(in_order(here) + in_order(other))
    return multiply(blocks, c_mask.T, blank, n_a, n_b)


def solution(mesh):
    in_specs = (
        P(("row", "col", "layer"), None, None),
        P(("row", "col", "layer")),
        P(("row", "col", "layer"), None, None),
        P(("row", "col", "layer")),
        P("row", "col"),
    )
    out_specs = P(("row", "layer"), "col")
    return jax.shard_map(
        on_device, mesh=mesh, in_specs=in_specs, out_specs=out_specs, check_vma=False
    )
```
